32 devices in a mesh: lev: 2 (over x), gx: 8 (over z, y), gy: 2 (over core).
Axes of the slice: x: 2, y: 2, z: 4, core: 2. Of those that a mesh axis runs over, the one named last changes fastest.
Arguments:
- increments: float32 [1, 2, 80, 128, 256], P(None, None, 'lev', 'gx', 'gy'), may hold values from -6 to 6
- vert_corr: float32 [2, 80, 80], replicated, may hold values from -0.025 to 1, as said below
- kappa: float32 [2, 128, 256], P(None, 'gx', 'gy'), may hold values from 0.03 to 0.24
- sea_mask: int32 [80, 128, 256], P('lev', 'gx', 'gy'), may hold values 0 or 1
- level_count: int32 [128, 256], P('gx', 'gy'), may hold values from 10 to 75
Outputs:
- covaried: float32 [1, 2, 80, 128, 256], P(None, None, 'lev', 'gx', 'gy')
The draws below stay inside these ranges and needn't reach their ends.
Inputs may be any that keep to these rules, and one draw needn't show every extreme that they name: vert_corr has ones on the diagonal, and each row's other entries together have magnitude below one.
All inputs are finite; a program needn't handle non-finite values. No bound on the sum of `sea_mask` on one device may be relied on, other than what follows from the above.
Results may differ from the reference program's by a relative error of at most 0.00021.
Values sent between devices are 32-bit elements; how exact they have to be, the bound alone decides.
A program may use at most 64 MiB of HBM per device.

```python
import math
import jax
import jax.numpy as jnp
from jax import lax

LEV = 80
TRACERS = 2
PASSES = 10
DIRS = 1
NX = 128
NY = 256


def draw_vert_corr(key, part):
    key_one = jax.random.fold_in(jax.random.fold_in(key, 17), 0)
    noise = jax.random.uniform(key_one, (TRACERS, LEV, LEV), jnp.float32, -1.0, 1.0)
    offdiag = noise * (1.2 / LEV)
    index = jnp.arange(LEV)
    diagonal = (index[:, None] == index[None, :])[None]
    return jnp.where(diagonal, 1.0, offdiag).astype(jnp.float32)


def plant(drawn, key, least, top_value):
    spot = [jax.random.randint(jax.random.fold_in(key, axis), (), 0, length) for axis, length in enumerate(drawn.shape)]
    widest = drawn.shape.index(max(drawn.shape))
    next_to = spot[:widest] + [(spot[widest] + 1) % drawn.shape[widest]] + spot[widest + 1:]
    return drawn.at[tuple(spot)].set(least).at[tuple(next_to)].set(top_value)


def shard_levels(stream_key, dims, shards, least, high):
    factor_of = 1.0
    for position, shards_of in shards:
        heights = jax.random.uniform(jax.random.fold_in(jax.random.fold_in(stream_key, 6), position), (shards_of,), jnp.float32, least / len(shards), high / len(shards))
        factor_of = factor_of * jnp.repeat(jnp.exp(heights), dims[position] // shards_of).reshape((-1,) + (1,) * (len(dims) - 1 - position))
    return factor_of


def normal_values(stream_key, dims, deviation, reach, cuts=(), held_as=jnp.bfloat16):
    loudness = shard_levels(stream_key, dims, cuts, -0.22, 0.18) if cuts else 1.0
    entries = jax.random.normal(stream_key, dims, jnp.float32) * deviation * loudness
    return jnp.minimum(jnp.maximum(entries, -reach), reach).astype(held_as)


def setup_inputs(seed: int = 0) -> dict:
    key_of = jax.random.split(jax.random.key(seed), 6)
    return {
        "increments": normal_values(key_of[0], (DIRS, TRACERS, LEV, NX, NY), 1.0, 6.0, ((2, 2), (3, 8), (4, 2)), jnp.float32),
        "vert_corr": draw_vert_corr(jax.random.fold_in(key_of[5], 71), 0),
        "kappa": jnp.clip(jnp.exp(math.log(0.24) - 2.0794415 * jax.random.uniform(key_of[2], (2, NX, NY), jnp.float32) ** shard_levels(key_of[2], (2, NX, NY), ((1, 8), (2, 2)), -0.2, 0.2)), 0.03, 0.24),
        "sea_mask": plant((jax.random.randint(key_of[3], (LEV, NX, NY), 0, 10) < 9).astype(jnp.int32), jax.random.fold_in(key_of[3], 1), 0, 1),
        "level_count": plant(jax.random.randint(key_of[4], (NX, NY), LEV // 8, LEV - LEV // 16 + 1), jax.random.fold_in(key_of[4], 1), LEV // 8, (LEV - LEV // 16 + 1) - 1).astype(jnp.int32),
    }


def reference(increments, vert_corr, kappa, sea_mask, level_count):
    levels = jnp.arange(LEV, dtype=jnp.int32)
    wet = (sea_mask * (levels[:, None, None] < level_count[None]).astype(jnp.int32)).astype(jnp.float32)
    east = kappa[0]
    north = kappa[1] * (jnp.arange(NY, dtype=jnp.int32) != NY - 1).astype(jnp.float32)[None, :]
    east_back = jnp.roll(east, 1, 0)
    north_back = jnp.roll(north, 1, 1)
    fields = increments.reshape(DIRS * TRACERS, LEV, NX, NY)
    tracer_ids = jnp.tile(jnp.arange(TRACERS, dtype=jnp.int32), DIRS)

    def apply_one(item):
        field, tracer = item
        matrix = vert_corr[tracer]
        masked = field * wet
        result = jnp.einsum("oh,hxy->oxy", matrix, masked, precision=lax.Precision.HIGHEST) * wet
        for step in range(PASSES):
            flux = east * (jnp.roll(result, -1, 1) - result) + east_back * (jnp.roll(result, 1, 1) - result)
            flux = flux + north * (jnp.roll(result, -1, 2) - result) + north_back * (jnp.roll(result, 1, 2) - result)
            result = wet * (result + flux)
        return result

    output = lax.map(apply_one, (fields, tracer_ids))
    return output.reshape(increments.shape)
```

```python
import jax
import jax.numpy as jnp
from jax import lax
from jax.experimental import pallas as pl
from jax.experimental.pallas import tpu as pltpu
from jax.sharding import PartitionSpec as P

PASSES = 10


def from_behind(block, axis, distance):
    devices = range(lax.axis_size(axis))
    route = [((i - distance) % len(devices), i) for i in devices]
    return lax.ppermute(block, axis, route)


def shifted(block, axis, distance):
    devices = range(lax.axis_size(axis))
    route = [(i - distance, i) for i in devices if i - distance in devices]
    return lax.ppermute(block, axis, route)


def padded(cells, sides, width):
    for axis, dim in sides:
        count = lax.axis_size(axis)
        head = lax.slice_in_dim(cells, 0, width, axis=dim)
        tail = lax.slice_in_dim(cells, cells.shape[dim] - width, cells.shape[dim], axis=dim)
        cells = jnp.concatenate(
            [
                lax.ppermute(tail, axis, [(i, (i + 1) % count) for i in range(count)]),
                cells,
                lax.ppermute(head, axis, [((i + 1) % count, i) for i in range(count)]),
            ],
            axis=dim,
        )
    return cells


def relax(extended, east_ext, north_ext, wet_center):
    center = extended[..., 1:-1, 1:-1]
    flux = east_ext[1:-1, 1:-1] * (extended[..., 2:, 1:-1] - center)
    flux = flux + east_ext[:-2, 1:-1] * (extended[..., :-2, 1:-1] - center)
    flux = flux + north_ext[1:-1, 1:-1] * (extended[..., 1:-1, 2:] - center)
    flux = flux + north_ext[1:-1, :-2] * (extended[..., 1:-1, :-2] - center)
    return wet_center * (center + flux)


def per_device(increments, vert_corr, kappa, sea_mask, level_count):
    lev_dev = sea_mask.shape[0]
    cells_x = sea_mask.shape[1]
    cells_y = sea_mask.shape[2]
    lev_first = lax.axis_index("lev") * lev_dev
    levels = lev_first + jnp.arange(lev_dev, dtype=jnp.int32)
    wet = sea_mask * (levels[:, None, None] < level_count[None]).astype(jnp.int32)
    wet_float = wet.astype(jnp.float32)
    masked = increments * wet_float
    own_rows = lax.dynamic_slice_in_dim(vert_corr, lev_first, lev_dev, 1)
    correlated = jnp.einsum(
        "toh,dthxy->dtoxy",
        own_rows,
        lax.all_gather(masked, "lev", axis=2, tiled=True),
        precision=lax.Precision.HIGHEST,
    )
    field = correlated * wet_float
    total_y = cells_y * lax.axis_size("gy")
    local_rows = lax.axis_index("gy") * cells_y + jnp.arange(cells_y, dtype=jnp.int32)
    open_local = (local_rows != total_y - 1).astype(jnp.float32)
    east_local = kappa[0]
    north_local = kappa[1] * open_local[None, :]
    east_low = from_behind(east_local[-1:, :], "gx", 1)
    north_low = shifted(north_local[:, -1:], "gy", 1)
    zero_row = jnp.zeros((1, cells_y), jnp.float32)
    zero_col = jnp.zeros((cells_x, 1), jnp.float32)
    east_ext = jnp.pad(jnp.concatenate([east_low, east_local, zero_row], axis=0), ((0, 0), (1, 1)))
    north_ext = jnp.pad(
        jnp.concatenate([north_low, north_local, zero_col], axis=1), ((1, 1), (0, 0))
    )

    def one_pass(step, current):
        extended = padded(current, (("gx", 3), ("gy", 4)), 1)
        return relax(extended, east_ext, north_ext, wet_float)

    field = lax.fori_loop(0, PASSES, one_pass, field)
    return field


TILE = 8
LANES = 128
WIDTH = 5
PARTS = 4
MESH = pl.DeviceIdType.MESH


def remote(src, dst, send_sem, recv_sem, device):
    return pltpu.make_async_remote_copy(
        src_ref=src,
        dst_ref=dst,
        send_sem=send_sem,
        recv_sem=recv_sem,
        device_id=device,
        device_id_type=MESH,
    )


def kernel(
    masked_ref, geo_ref, corr_ref, out_ref,
    geo, own, other, field, halo, east, north,
    own_sems, same_sems, cross_sems, geo_sems, halo_sems, out_sems,
):
    lev, gx, gy = lax.axis_index("lev"), lax.axis_index("gx"), lax.axis_index("gy")
    count = lax.axis_size("gx")
    cells = masked_ref.shape[1]
    levels = masked_ref.shape[2]
    tiles = levels // TILE
    width = WIDTH
    rows = cells + 2 * width
    rounds = PASSES // width
    east_dev = {"gx": lax.rem(gx + 1, count)}
    west_dev = {"gx": lax.rem(gx + count - 1, count)}
    mate = {"gy": 1 - gy}
    pair = {"lev": 1 - lev}
    cross = {"lev": 1 - lev, "gy": 1 - gy}

    barrier = pltpu.get_barrier_semaphore()
    everyone = (east_dev, west_dev, mate, pair, cross)
    for device in everyone:
        pl.semaphore_signal(barrier, inc=1, device_id=device, device_id_type=MESH)
    pl.semaphore_wait(barrier, len(everyone))

    part = cells // PARTS
    spans = [pl.ds(q * part, part) for q in range(PARTS)]
    own_copies, same_copies, cross_copies = [], [], []
    order = [0, PARTS - 1] + list(range(1, PARTS - 1))
    for q in order:
        same_copies.append(remote(
            masked_ref.at[gy, spans[q]], other.at[gy, spans[q]],
            same_sems.at[0, q], same_sems.at[1, q], pair))
        cross_copies.append(remote(
            masked_ref.at[1 - gy, spans[q]], other.at[gy, spans[q]],
            cross_sems.at[0, q], cross_sems.at[1, q], cross))
        same_copies[-1].start()
        cross_copies[-1].start()
    geo_copies = [
        remote(geo_ref, geo.at[gy, pl.ds(width, cells)], geo_sems.at[0, 0], geo_sems.at[1, 0], mate),
        remote(geo_ref.at[pl.ds(cells - width, width)], geo.at[gy, pl.ds(0, width)],
               geo_sems.at[0, 1], geo_sems.at[1, 1], east_dev),
        remote(geo_ref.at[pl.ds(0, width)], geo.at[gy, pl.ds(width + cells, width)],
               geo_sems.at[0, 2], geo_sems.at[1, 2], west_dev),
    ]
    for copy in geo_copies:
        copy.start()
    own_copy = remote(masked_ref.at[1 - gy], own, own_sems.at[0], own_sems.at[1], mate)
    own_copy.start()

    geo[gy, width:width + cells] = geo_ref[...]
    corr = corr_ref[...]
    high = corr.astype(jnp.bfloat16)
    low = (corr - high.astype(jnp.float32)).astype(jnp.bfloat16)
    weights = jnp.concatenate([high, high, low], axis=1)

    own_copy.wait()
    geo_copies[0].wait()
    forward = []
    for side, start in ((1, 0), (2, width + cells)):
        geo_copies[side].wait()
        forward.append(remote(
            geo.at[gy, pl.ds(start, width)], geo.at[gy, pl.ds(start, width)],
            geo_sems.at[0, 2 + side], geo_sems.at[1, 2 + side], mate))
        forward[-1].start()

    def send_halo(r, k):
        copies = (
            remote(field.at[k, pl.ds(width, width)], halo.at[r, 1, k],
                   halo_sems.at[0, r, 0, k], halo_sems.at[1, r, 0, k], west_dev),
            remote(field.at[k, pl.ds(cells, width)], halo.at[r, 0, k],
                   halo_sems.at[0, r, 1, k], halo_sems.at[1, r, 1, k], east_dev),
        )
        for copy in copies:
            copy.start()
        return copies

    def vertical(x):
        mine = masked_ref[gy, x]
        theirs = own[x]
        first = jnp.where(gy == 0, mine, theirs)
        second = jnp.where(gy == 0, theirs, mine)
        near = jnp.concatenate([first, second], axis=1)
        far = jnp.concatenate([other[0, x], other[1, x]], axis=1)
        both = jnp.concatenate([near, far], axis=0)
        top = both.astype(jnp.bfloat16)
        rest = (both - top.astype(jnp.float32)).astype(jnp.bfloat16)
        stack = jnp.concatenate([top, rest, top], axis=0)
        result = jnp.dot(weights, stack, preferred_element_type=jnp.float32)
        for half in range(2):
            for k in range(tiles):
                value = result[k * TILE:(k + 1) * TILE, half * LANES:(half + 1) * LANES]
                wet = geo[half, width + x, k * TILE:(k + 1) * TILE]
                field[k, width + x, half] = value * wet

    for place, q in enumerate(order):
        same_copies[place].wait()
        cross_copies[place].wait()
        for x in range(q * part, (q + 1) * part):
            vertical(x)

    pending = [send_halo(0, k) for k in range(tiles)]

    for copy in forward:
        copy.wait()
    for half in range(2):
        for row in range(rows):
            east[row, half] = jnp.broadcast_to(geo[half, row, levels:levels + 1], (TILE, LANES))
            north[row, half] = jnp.broadcast_to(geo[half, row, levels + 1:levels + 2], (TILE, LANES))

    lane = lax.broadcasted_iota(jnp.int32, (TILE, LANES), 1)
    at_end = lane == LANES - 1
    at_start = lane == 0

    def relax_tile(r, k):
        for step in range(width):
            def row_of(row):
                if step == 0 and row < width:
                    return halo[r, 0, k, row, 0], halo[r, 0, k, row, 1]
                if step == 0 and row >= width + cells:
                    at = row - width - cells
                    return halo[r, 1, k, at, 0], halo[r, 1, k, at, 1]
                return field[k, row, 0], field[k, row, 1]

            first, last = step + 1, rows - 2 - step
            before, here = row_of(first - 1), row_of(first)
            flux = [east[first - 1, h] * (here[h] - before[h]) for h in range(2)]
            for row in range(first, last + 1):
                after = row_of(row + 1)
                turned = [pltpu.roll(here[h], LANES - 1, 1) for h in range(2)]
                up = [jnp.where(at_end, turned[1], turned[0]), turned[1]]
                rise = [north[row, h] * (up[h] - here[h]) for h in range(2)]
                back = [pltpu.roll(rise[h], 1, 1) for h in range(2)]
                down = [jnp.where(at_start, back[1], back[0]), jnp.where(at_start, back[0], back[1])]
                ahead = [east[row, h] * (after[h] - here[h]) for h in range(2)]
                for h in range(2):
                    wet = geo[h, row, k * TILE:(k + 1) * TILE]
                    total = here[h] + ((ahead[h] - flux[h]) + (rise[h] - down[h]))
                    field[k, row, h] = wet * total
                here, flux = after, ahead

    out_copies = []
    for r in range(rounds):
        later = []
        for k in range(tiles):
            for copy in pending[k]:
                copy.wait()
            relax_tile(r, k)
            if r < rounds - 1:
                later.append(send_halo(r + 1, k))
            else:
                out_copies.append(remote(
                    field.at[k, pl.ds(width, cells), 1 - gy], out_ref.at[gy, k],
                    out_sems.at[0, k], out_sems.at[1, k], mate))
                out_copies[-1].start()
                out_ref[gy, k] = field[k, width:width + cells, gy]
        pending = later
    for copy in out_copies:
        copy.wait()


def fused(increments, vert_corr, kappa, sea_mask, level_count):
    levels, cells, lanes = sea_mask.shape
    tiles = levels // TILE
    width = WIDTH
    rows = cells + 2 * width
    rounds = PASSES // width
    gy = lax.axis_index("gy")
    lev = lax.axis_index("lev")
    numbers = lev * levels + jnp.arange(levels, dtype=jnp.int32)
    turned = jnp.swapaxes(sea_mask, 0, 1)
    wet = (turned * (numbers[None, :, None] < level_count[:, None, :]).astype(jnp.int32)).astype(jnp.float32)
    masked = jnp.swapaxes(increments[0], 1, 2) * wet[None]
    total_y = lanes * lax.axis_size("gy")
    local_rows = gy * lanes + jnp.arange(lanes, dtype=jnp.int32)
    north = kappa[1] * (local_rows != total_y - 1).astype(jnp.float32)[None]
    fill = jnp.zeros((cells, TILE - 2, lanes), jnp.float32)
    geo = jnp.concatenate([wet, kappa[0][:, None], north[:, None], fill], axis=1)
    mine = lax.dynamic_slice(vert_corr, (gy, lev * levels, 0), (1, levels, 2 * levels))[0]
    corr = jnp.where(lev == 0, mine, jnp.roll(mine, levels, 1))
    vmem = pl.BlockSpec(memory_space=pltpu.VMEM)
    f32 = jnp.float32
    dma = pltpu.SemaphoreType.DMA
    result = pl.pallas_call(
        kernel,
        out_shape=jax.ShapeDtypeStruct((2, tiles, cells, TILE, lanes), f32),
        in_specs=[vmem] * 3,
        out_specs=vmem,
        scratch_shapes=[
            pltpu.VMEM((2, rows, levels + TILE, lanes), f32),
            pltpu.VMEM((cells, levels, lanes), f32),
            pltpu.VMEM((2, cells, levels, lanes), f32),
            pltpu.VMEM((tiles, rows, 2, TILE, lanes), f32),
            pltpu.VMEM((rounds, 2, tiles, width, 2, TILE, lanes), f32),
            pltpu.VMEM((rows, 2, TILE, lanes), f32),
            pltpu.VMEM((rows, 2, TILE, lanes), f32),
            dma((2,)),
            dma((2, PARTS)),
            dma((2, PARTS)),
            dma((2, 5)),
            dma((2, rounds, 2, tiles)),
            dma((2, tiles)),
        ],
        compiler_params=pltpu.CompilerParams(
            collective_id=0, has_side_effects=True, vmem_limit_bytes=32 * 1024 * 1024
        ),
        cost_estimate=pl.CostEstimate(flops=60_000_000, bytes_accessed=4_000_000, transcendentals=0),
    )(masked, geo, corr)
    return result.transpose(0, 1, 3, 2, 4).reshape(increments.shape)


def fits(mesh):
    shape = mesh.shape
    return shape["lev"] == 2 and shape["gy"] == 2 and shape["gx"] > 2


def solution(mesh):
    in_specs = (
        P(None, None, "lev", "gx", "gy"),
        P(),
        P(None, "gx", "gy"),
        P("lev", "gx", "gy"),
        P("gx", "gy"),
    )
    out_specs = P(None, None, "lev", "gx", "gy")
    return jax.shard_map(
        fused if fits(mesh) else per_device, mesh=mesh, in_specs=in_specs, out_specs=out_specs, check_vma=False
    )
```

```python
import jax
import jax.numpy as jnp
from jax import lax
from jax.experimental import pallas as pl
from jax.experimental.pallas import tpu as pltpu
from jax.sharding import PartitionSpec as P

PASSES = 10


def from_behind(block, axis, distance):
    devices = range(lax.axis_size(axis))
    route = [((i - distance) % len(devices), i) for i in devices]
    return lax.ppermute(block, axis, route)


def shifted(block, axis, distance):
    devices = range(lax.axis_size(axis))
    route = [(i - distance, i) for i in devices if i - distance in devices]
    return lax.ppermute(block, axis, route)


def padded(cells, sides, width):
    for axis, dim in sides:
        count = lax.axis_size(axis)
        head = lax.slice_in_dim(cells, 0, width, axis=dim)
        tail = lax.slice_in_dim(cells, cells.shape[dim] - width, cells.shape[dim], axis=dim)
        cells = jnp.concatenate(
            [
                lax.ppermute(tail, axis, [(i, (i + 1) % count) for i in range(count)]),
                cells,
                lax.ppermute(head, axis, [((i + 1) % count, i) for i in range(count)]),
            ],
            axis=dim,
        )
    return cells


def relax(extended, east_ext, north_ext, wet_center):
    center = extended[..., 1:-1, 1:-1]
    flux = east_ext[1:-1, 1:-1] * (extended[..., 2:, 1:-1] - center)
    flux = flux + east_ext[:-2, 1:-1] * (extended[..., :-2, 1:-1] - center)
    flux = flux + north_ext[1:-1, 1:-1] * (extended[..., 1:-1, 2:] - center)
    flux = flux + north_ext[1:-1, :-2] * (extended[..., 1:-1, :-2] - center)
    return wet_center * (center + flux)


def per_device(increments, vert_corr, kappa, sea_mask, level_count):
    lev_dev = sea_mask.shape[0]
    cells_x = sea_mask.shape[1]
    cells_y = sea_mask.shape[2]
    lev_first = lax.axis_index("lev") * lev_dev
    levels = lev_first + jnp.arange(lev_dev, dtype=jnp.int32)
    wet = sea_mask * (levels[:, None, None] < level_count[None]).astype(jnp.int32)
    wet_float = wet.astype(jnp.float32)
    masked = increments * wet_float
    own_rows = lax.dynamic_slice_in_dim(vert_corr, lev_first, lev_dev, 1)
    correlated = jnp.einsum(
        "toh,dthxy->dtoxy",
        own_rows,
        lax.all_gather(masked, "lev", axis=2, tiled=True),
        precision=lax.Precision.HIGHEST,
    )
    field = correlated * wet_float
    total_y = cells_y * lax.axis_size("gy")
    local_rows = lax.axis_index("gy") * cells_y + jnp.arange(cells_y, dtype=jnp.int32)
    open_local = (local_rows != total_y - 1).astype(jnp.float32)
    east_local = kappa[0]
    north_local = kappa[1] * open_local[None, :]
    east_low = from_behind(east_local[-1:, :], "gx", 1)
    north_low = shifted(north_local[:, -1:], "gy", 1)
    zero_row = jnp.zeros((1, cells_y), jnp.float32)
    zero_col = jnp.zeros((cells_x, 1), jnp.float32)
    east_ext = jnp.pad(jnp.concatenate([east_low, east_local, zero_row], axis=0), ((0, 0), (1, 1)))
    north_ext = jnp.pad(
        jnp.concatenate([north_low, north_local, zero_col], axis=1), ((1, 1), (0, 0))
    )

    def one_pass(step, current):
        extended = padded(current, (("gx", 3), ("gy", 4)), 1)
        return relax(extended, east_ext, north_ext, wet_float)

    field = lax.fori_loop(0, PASSES, one_pass, field)
    return field


TILE = 8
LANES = 128
WIDTH = 5
MESH = pl.DeviceIdType.MESH


def remote(src, dst, send_sem, recv_sem, device):
    return pltpu.make_async_remote_copy(
        src_ref=src,
        dst_ref=dst,
        send_sem=send_sem,
        recv_sem=recv_sem,
        device_id=device,
        device_id_type=MESH,
    )


def kernel(
    masked_ref, geo_ref, corr_ref, out_ref,
    geo, own, other, field, halo, east, north,
    own_sems, same_sems, cross_sems, geo_sems, halo_sems, out_sems,
):
    lev, gx, gy = lax.axis_index("lev"), lax.axis_index("gx"), lax.axis_index("gy")
    count = lax.axis_size("gx")
    cells = masked_ref.shape[1]
    levels = masked_ref.shape[2]
    tiles = levels // TILE
    width = WIDTH
    rows = cells + 2 * width
    rounds = PASSES // width
    east_dev = {"gx": lax.rem(gx + 1, count)}
    west_dev = {"gx": lax.rem(gx + count - 1, count)}
    mate = {"gy": 1 - gy}
    pair = {"lev": 1 - lev}
    cross = {"lev": 1 - lev, "gy": 1 - gy}

    barrier = pltpu.get_barrier_semaphore()
    everyone = (east_dev, west_dev, mate, pair, cross)
    for device in everyone:
        pl.semaphore_signal(barrier, inc=1, device_id=device, device_id_type=MESH)
    pl.semaphore_wait(barrier, len(everyone))

    starts = ((0, width), (cells - width, width), (width, cells - 2 * width))
    own_copies, same_copies, cross_copies = [], [], []
    for q, (start, size) in enumerate(starts):
        span = pl.ds(start, size)
        own_copies.append(remote(
            masked_ref.at[1 - gy, span], own.at[span], own_sems.at[0, q], own_sems.at[1, q], mate))
        same_copies.append(remote(
            masked_ref.at[gy, span], other.at[gy, span],
            same_sems.at[0, q], same_sems.at[1, q], pair))
        cross_copies.append(remote(
            masked_ref.at[1 - gy, span], other.at[gy, span],
            cross_sems.at[0, q], cross_sems.at[1, q], cross))
    geo_copies = [
        remote(geo_ref, geo.at[gy, pl.ds(width, cells)], geo_sems.at[0, 0], geo_sems.at[1, 0], mate),
        remote(geo_ref.at[pl.ds(cells - width, width)],
               geo.at[gy, pl.ds(0, width)],
               geo_sems.at[0, 1], geo_sems.at[1, 1], east_dev),
        remote(geo_ref.at[pl.ds(0, width)],
               geo.at[gy, pl.ds(width + cells, width)],
               geo_sems.at[0, 2], geo_sems.at[1, 2], west_dev),
    ]
    for q in range(len(starts)):
        same_copies[q].start()
        cross_copies[q].start()
        if q == 0:
            for copy in geo_copies[1:]:
                copy.start()
            geo_copies[0].start()
        own_copies[q].start()

    geo[gy, width:width + cells] = geo_ref[...]
    corr = corr_ref[...]
    high = corr.astype(jnp.bfloat16)
    low = (corr - high.astype(jnp.float32)).astype(jnp.bfloat16)
    weights = jnp.concatenate([high, high, low], axis=1)

    def halo_copies(r, k):
        return (
            remote(field.at[k, pl.ds(width, width)], halo.at[r, 1, k],
                   halo_sems.at[0, r, 0, k], halo_sems.at[1, r, 0, k], west_dev),
            remote(field.at[k, pl.ds(cells, width)], halo.at[r, 0, k],
                   halo_sems.at[0, r, 1, k], halo_sems.at[1, r, 1, k], east_dev),
        )

    def vertical(x):
        mine = masked_ref[gy, x]
        theirs = own[x]
        first = jnp.where(gy == 0, mine, theirs)
        second = jnp.where(gy == 0, theirs, mine)
        near = jnp.concatenate([first, second], axis=1)
        far = jnp.concatenate([other[0, x], other[1, x]], axis=1)
        both = jnp.concatenate([near, far], axis=0)
        top = both.astype(jnp.bfloat16)
        rest = (both - top.astype(jnp.float32)).astype(jnp.bfloat16)
        stack = jnp.concatenate([top, rest, top], axis=0)
        result = jnp.dot(weights, stack, preferred_element_type=jnp.float32)
        for half in range(2):
            for k in range(tiles):
                value = result[k * TILE:(k + 1) * TILE, half * LANES:(half + 1) * LANES]
                wet = geo[half, width + x, k * TILE:(k + 1) * TILE]
                field[k, width + x, half] = value * wet

    pending = [halo_copies(0, k) for k in range(tiles)]
    forward = []
    geo_copies[0].wait()
    for q, (start, size) in enumerate(starts):
        own_copies[q].wait()
        same_copies[q].wait()
        cross_copies[q].wait()
        for x in range(start, start + size):
            vertical(x)
        if q < 2:
            for k in range(tiles):
                pending[k][q].start()
        if q == 1:
            for side, place in ((1, 0), (2, width + cells)):
                geo_copies[side].wait()
                edge = geo.at[gy, pl.ds(place, width)]
                forward.append(remote(
                    edge, edge, geo_sems.at[0, 2 + side], geo_sems.at[1, 2 + side], mate))
                forward[-1].start()
    for copy in forward:
        copy.wait()
    for half in range(2):
        for row in range(rows):
            east[row, half] = jnp.broadcast_to(geo[half, row, levels:levels + 1], (TILE, LANES))
            north[row, half] = jnp.broadcast_to(geo[half, row, levels + 1:levels + 2], (TILE, LANES))

    lane = lax.broadcasted_iota(jnp.int32, (TILE, LANES), 1)
    at_end = lane == LANES - 1
    at_start = lane == 0

    def relax_tile(r, k):
        for step in range(width):
            def row_of(row):
                if step == 0 and row < width:
                    return halo[r, 0, k, row, 0], halo[r, 0, k, row, 1]
                if step == 0 and row >= width + cells:
                    at = row - width - cells
                    return halo[r, 1, k, at, 0], halo[r, 1, k, at, 1]
                return field[k, row, 0], field[k, row, 1]

            first, last = step + 1, rows - 2 - step
            before, here = row_of(first - 1), row_of(first)
            flux = [east[first - 1, h] * (here[h] - before[h]) for h in range(2)]
            for row in range(first, last + 1):
                after = row_of(row + 1)
                turned = [pltpu.roll(here[h], LANES - 1, 1) for h in range(2)]
                up = [jnp.where(at_end, turned[1], turned[0]), turned[1]]
                rise = [north[row, h] * (up[h] - here[h]) for h in range(2)]
                back = [pltpu.roll(rise[h], 1, 1) for h in range(2)]
                down = [jnp.where(at_start, back[1], back[0]), jnp.where(at_start, back[0], back[1])]
                ahead = [east[row, h] * (after[h] - here[h]) for h in range(2)]
                for h in range(2):
                    wet = geo[h, row, k * TILE:(k + 1) * TILE]
                    total = here[h] + ((ahead[h] - flux[h]) + (rise[h] - down[h]))
                    field[k, row, h] = wet * total
                here, flux = after, ahead

    out_copies = []
    for r in range(rounds):
        later = []
        for k in range(tiles):
            for copy in pending[k]:
                copy.wait()
            relax_tile(r, k)
            if r < rounds - 1:
                later.append(halo_copies(r + 1, k))
                for copy in later[-1]:
                    copy.start()
            else:
                out_copies.append(remote(
                    field.at[k, pl.ds(width, cells), 1 - gy], out_ref.at[gy, k],
                    out_sems.at[0, k], out_sems.at[1, k], mate))
                out_copies[-1].start()
                out_ref[gy, k] = field[k, width:width + cells, gy]
        pending = later
    for copy in out_copies:
        copy.wait()


def fused(increments, vert_corr, kappa, sea_mask, level_count):
    levels, cells, lanes = sea_mask.shape
    tiles = levels // TILE
    width = WIDTH
    rows = cells + 2 * width
    rounds = PASSES // width
    gy = lax.axis_index("gy")
    lev = lax.axis_index("lev")
    numbers = lev * levels + jnp.arange(levels, dtype=jnp.int32)
    turned = jnp.swapaxes(sea_mask, 0, 1)
    wet = (turned * (numbers[None, :, None] < level_count[:, None, :]).astype(jnp.int32)).astype(jnp.float32)
    masked = jnp.swapaxes(increments[0], 1, 2) * wet[None]
    total_y = lanes * lax.axis_size("gy")
    local_rows = gy * lanes + jnp.arange(lanes, dtype=jnp.int32)
    north = kappa[1] * (local_rows != total_y - 1).astype(jnp.float32)[None]
    fill = jnp.zeros((cells, TILE - 2, lanes), jnp.float32)
    geo = jnp.concatenate([wet, kappa[0][:, None], north[:, None], fill], axis=1)
    mine = lax.dynamic_slice(vert_corr, (gy, lev * levels, 0), (1, levels, 2 * levels))[0]
    corr = jnp.where(lev == 0, mine, jnp.roll(mine, levels, 1))
    vmem = pl.BlockSpec(memory_space=pltpu.VMEM)
    f32 = jnp.float32
    dma = pltpu.SemaphoreType.DMA
    result = pl.pallas_call(
        kernel,
        out_shape=jax.ShapeDtypeStruct((2, tiles, cells, TILE, lanes), f32),
        in_specs=[vmem] * 3,
        out_specs=vmem,
        scratch_shapes=[
            pltpu.VMEM((2, rows, levels + TILE, lanes), f32),
            pltpu.VMEM((cells, levels, lanes), f32),
            pltpu.VMEM((2, cells, levels, lanes), f32),
            pltpu.VMEM((tiles, rows, 2, TILE, lanes), f32),
            pltpu.VMEM((rounds, 2, tiles, width, 2, TILE, lanes), f32),
            pltpu.VMEM((rows, 2, TILE, lanes), f32),
            pltpu.VMEM((rows, 2, TILE, lanes), f32),
            dma((2, 3)),
            dma((2, 3)),
            dma((2, 3)),
            dma((2, 5)),
            dma((2, rounds, 2, tiles)),
            dma((2, tiles)),
        ],
        compiler_params=pltpu.CompilerParams(
            collective_id=0, has_side_effects=True, vmem_limit_bytes=32 * 1024 * 1024
        ),
        cost_estimate=pl.CostEstimate(flops=60_000_000, bytes_accessed=4_000_000, transcendentals=0),
    )(masked, geo, corr)
    return result.transpose(0, 1, 3, 2, 4).reshape(increments.shape)


def fits(mesh):
    shape = mesh.shape
    return shape["lev"] == 2 and shape["gy"] == 2 and shape["gx"] > 2


def solution(mesh):
    in_specs = (
        P(None, None, "lev", "gx", "gy"),
        P(),
        P(None, "gx", "gy"),
        P("lev", "gx", "gy"),
        P("gx", "gy"),
    )
    out_specs = P(None, None, "lev", "gx", "gy")
    return jax.shard_map(
        fused if fits(mesh) else per_device, mesh=mesh, in_specs=in_specs, out_specs=out_specs, check_vma=False
    )
```

```python
import jax
import jax.numpy as jnp
from jax import lax
from jax.experimental import pallas as pl
from jax.experimental.pallas import tpu as pltpu
from jax.sharding import PartitionSpec as P

PASSES = 10


def from_behind(block, axis, distance):
    devices = range(lax.axis_size(axis))
    route = [((i - distance) % len(devices), i) for i in devices]
    return lax.ppermute(block, axis, route)


def shifted(block, axis, distance):
    devices = range(lax.axis_size(axis))
    route = [(i - distance, i) for i in devices if i - distance in devices]
    return lax.ppermute(block, axis, route)


def padded(cells, sides, width):
    for axis, dim in sides:
        count = lax.axis_size(axis)
        head = lax.slice_in_dim(cells, 0, width, axis=dim)
        tail = lax.slice_in_dim(cells, cells.shape[dim] - width, cells.shape[dim], axis=dim)
        cells = jnp.concatenate(
            [
                lax.ppermute(tail, axis, [(i, (i + 1) % count) for i in range(count)]),
                cells,
                lax.ppermute(head, axis, [((i + 1) % count, i) for i in range(count)]),
            ],
            axis=dim,
        )
    return cells


def relax(extended, east_ext, north_ext, wet_center):
    center = extended[..., 1:-1, 1:-1]
    flux = east_ext[1:-1, 1:-1] * (extended[..., 2:, 1:-1] - center)
    flux = flux + east_ext[:-2, 1:-1] * (extended[..., :-2, 1:-1] - center)
    flux = flux + north_ext[1:-1, 1:-1] * (extended[..., 1:-1, 2:] - center)
    flux = flux + north_ext[1:-1, :-2] * (extended[..., 1:-1, :-2] - center)
    return wet_center * (center + flux)


def per_device(increments, vert_corr, kappa, sea_mask, level_count):
    lev_dev = sea_mask.shape[0]
    cells_x = sea_mask.shape[1]
    cells_y = sea_mask.shape[2]
    lev_first = lax.axis_index("lev") * lev_dev
    levels = lev_first + jnp.arange(lev_dev, dtype=jnp.int32)
    wet = sea_mask * (levels[:, None, None] < level_count[None]).astype(jnp.int32)
    wet_float = wet.astype(jnp.float32)
    masked = increments * wet_float
    own_rows = lax.dynamic_slice_in_dim(vert_corr, lev_first, lev_dev, 1)
    correlated = jnp.einsum(
        "toh,dthxy->dtoxy",
        own_rows,
        lax.all_gather(masked, "lev", axis=2, tiled=True),
        precision=lax.Precision.HIGHEST,
    )
    field = correlated * wet_float
    total_y = cells_y * lax.axis_size("gy")
    local_rows = lax.axis_index("gy") * cells_y + jnp.arange(cells_y, dtype=jnp.int32)
    open_local = (local_rows != total_y - 1).astype(jnp.float32)
    east_local = kappa[0]
    north_local = kappa[1] * open_local[None, :]
    east_low = from_behind(east_local[-1:, :], "gx", 1)
    north_low = shifted(north_local[:, -1:], "gy", 1)
    zero_row = jnp.zeros((1, cells_y), jnp.float32)
    zero_col = jnp.zeros((cells_x, 1), jnp.float32)
    east_ext = jnp.pad(jnp.concatenate([east_low, east_local, zero_row], axis=0), ((0, 0), (1, 1)))
    north_ext = jnp.pad(
        jnp.concatenate([north_low, north_local, zero_col], axis=1), ((1, 1), (0, 0))
    )

    def one_pass(step, current):
        extended = padded(current, (("gx", 3), ("gy", 4)), 1)
        return relax(extended, east_ext, north_ext, wet_float)

    field = lax.fori_loop(0, PASSES, one_pass, field)
    return field


TILE = 8
LANES = 128
WIDTH = 5
MESH = pl.DeviceIdType.MESH


def remote(src, dst, send_sem, recv_sem, device):
    return pltpu.make_async_remote_copy(
        src_ref=src,
        dst_ref=dst,
        send_sem=send_sem,
        recv_sem=recv_sem,
        device_id=device,
        device_id_type=MESH,
    )


def kernel(
    masked_ref, wet_ref, corr_ref, kappa_ref, out_ref,
    geo, own, other, field, halo, east, north,
    own_sems, same_sems, cross_sems, geo_sems, halo_sems, out_sems,
):
    lev, gx, gy = lax.axis_index("lev"), lax.axis_index("gx"), lax.axis_index("gy")
    count = lax.axis_size("gx")
    cells = masked_ref.shape[1]
    levels = masked_ref.shape[2]
    lanes = masked_ref.shape[3]
    tiles = levels // TILE
    width = WIDTH
    rows = cells + 2 * width
    rounds = PASSES // width
    east_dev = {"gx": lax.rem(gx + 1, count)}
    west_dev = {"gx": lax.rem(gx + count - 1, count)}
    mate = {"gy": 1 - gy}
    pair = {"lev": 1 - lev}
    cross = {"lev": 1 - lev, "gy": 1 - gy}

    barrier = pltpu.get_barrier_semaphore()
    everyone = (east_dev, west_dev, mate, pair, cross)
    for device in everyone:
        pl.semaphore_signal(barrier, inc=1, device_id=device, device_id_type=MESH)
    columns = gy * lanes + lax.broadcasted_iota(jnp.int32, (1, lanes), 1)
    is_open = (columns != lanes * lax.axis_size("gy") - 1).astype(jnp.float32)
    geo[gy, width:width + cells, 0:levels] = wet_ref[...]
    for x in range(cells):
        geo[gy, width + x, levels:levels + 1] = kappa_ref[0, x:x + 1]
        geo[gy, width + x, levels + 1:levels + 2] = kappa_ref[1, x:x + 1] * is_open
        geo[gy, width + x, levels + 2:] = jnp.zeros((TILE - 2, lanes), jnp.float32)
    pl.semaphore_wait(barrier, len(everyone))

    starts = ((0, width), (cells - width, width), (width, cells - 2 * width))
    own_copies, same_copies, cross_copies = [], [], []
    for q, (start, size) in enumerate(starts):
        span = pl.ds(start, size)
        own_copies.append(remote(
            masked_ref.at[1 - gy, span], own.at[span], own_sems.at[0, q], own_sems.at[1, q], mate))
        same_copies.append(remote(
            masked_ref.at[gy, span], other.at[gy, span],
            same_sems.at[0, q], same_sems.at[1, q], pair))
        cross_copies.append(remote(
            masked_ref.at[1 - gy, span], other.at[gy, span],
            cross_sems.at[0, q], cross_sems.at[1, q], cross))
    geo_copies = [
        remote(geo.at[gy, pl.ds(width, cells)], geo.at[gy, pl.ds(width, cells)], geo_sems.at[0, 0], geo_sems.at[1, 0], mate),
        remote(geo.at[gy, pl.ds(cells, width)],
               geo.at[gy, pl.ds(0, width)],
               geo_sems.at[0, 1], geo_sems.at[1, 1], east_dev),
        remote(geo.at[gy, pl.ds(width, width)],
               geo.at[gy, pl.ds(width + cells, width)],
               geo_sems.at[0, 2], geo_sems.at[1, 2], west_dev),
    ]
    for q in range(len(starts)):
        same_copies[q].start()
        cross_copies[q].start()
        if q == 0:
            for copy in geo_copies[1:]:
                copy.start()
            geo_copies[0].start()
        own_copies[q].start()

    mine = corr_ref[gy, pl.ds(pl.multiple_of(lev * levels, TILE), levels), :]
    swapped = jnp.concatenate([mine[:, levels:], mine[:, :levels]], axis=1)
    corr = jnp.where(lev == 0, mine, swapped)
    high = corr.astype(jnp.bfloat16)
    low = (corr - high.astype(jnp.float32)).astype(jnp.bfloat16)
    weights = jnp.concatenate([high, high, low], axis=1)

    def halo_copies(r, k):
        return (
            remote(field.at[k, pl.ds(width, width)], halo.at[r, 1, k],
                   halo_sems.at[0, r, 0, k], halo_sems.at[1, r, 0, k], west_dev),
            remote(field.at[k, pl.ds(cells, width)], halo.at[r, 0, k],
                   halo_sems.at[0, r, 1, k], halo_sems.at[1, r, 1, k], east_dev),
        )

    def vertical(x):
        mine = masked_ref[gy, x]
        theirs = own[x]
        first = jnp.where(gy == 0, mine, theirs)
        second = jnp.where(gy == 0, theirs, mine)
        near = jnp.concatenate([first, second], axis=1)
        far = jnp.concatenate([other[0, x], other[1, x]], axis=1)
        both = jnp.concatenate([near, far], axis=0)
        top = both.astype(jnp.bfloat16)
        rest = (both - top.astype(jnp.float32)).astype(jnp.bfloat16)
        stack = jnp.concatenate([top, rest, top], axis=0)
        result = jnp.dot(weights, stack, preferred_element_type=jnp.float32)
        for half in range(2):
            for k in range(tiles):
                value = result[k * TILE:(k + 1) * TILE, half * LANES:(half + 1) * LANES]
                wet = geo[half, width + x, k * TILE:(k + 1) * TILE]
                field[k, width + x, half] = value * wet

    pending = [halo_copies(0, k) for k in range(tiles)]
    forward = []
    geo_copies[0].wait()
    for q, (start, size) in enumerate(starts):
        own_copies[q].wait()
        same_copies[q].wait()
        cross_copies[q].wait()
        for x in range(start, start + size):
            vertical(x)
        if q < 2:
            for k in range(tiles):
                pending[k][q].start()
        if q == 1:
            for side, place in ((1, 0), (2, width + cells)):
                geo_copies[side].wait()
                edge = geo.at[gy, pl.ds(place, width)]
                forward.append(remote(
                    edge, edge, geo_sems.at[0, 2 + side], geo_sems.at[1, 2 + side], mate))
                forward[-1].start()
    for copy in forward:
        copy.wait()
    for half in range(2):
        for row in range(rows):
            east[row, half] = jnp.broadcast_to(geo[half, row, levels:levels + 1], (TILE, LANES))
            north[row, half] = jnp.broadcast_to(geo[half, row, levels + 1:levels + 2], (TILE, LANES))

    lane = lax.broadcasted_iota(jnp.int32, (TILE, LANES), 1)
    at_end = lane == LANES - 1
    at_start = lane == 0

    def relax_tile(r, k):
        for step in range(width):
            def row_of(row):
                if step == 0 and row < width:
                    return halo[r, 0, k, row, 0], halo[r, 0, k, row, 1]
                if step == 0 and row >= width + cells:
                    at = row - width - cells
                    return halo[r, 1, k, at, 0], halo[r, 1, k, at, 1]
                return field[k, row, 0], field[k, row, 1]

            first, last = step + 1, rows - 2 - step
            before, here = row_of(first - 1), row_of(first)
            flux = [east[first - 1, h] * (here[h] - before[h]) for h in range(2)]
            for row in range(first, last + 1):
                after = row_of(row + 1)
                turned = [pltpu.roll(here[h], LANES - 1, 1) for h in range(2)]
                up = [jnp.where(at_end, turned[1], turned[0]), turned[1]]
                rise = [north[row, h] * (up[h] - here[h]) for h in range(2)]
                back = [pltpu.roll(rise[h], 1, 1) for h in range(2)]
                down = [jnp.where(at_start, back[1], back[0]), jnp.where(at_start, back[0], back[1])]
                ahead = [east[row, h] * (after[h] - here[h]) for h in range(2)]
                for h in range(2):
                    wet = geo[h, row, k * TILE:(k + 1) * TILE]
                    total = here[h] + ((ahead[h] - flux[h]) + (rise[h] - down[h]))
                    field[k, row, h] = wet * total
                here, flux = after, ahead

    out_copies = []
    for r in range(rounds):
        later = []
        for k in range(tiles):
            for copy in pending[k]:
                copy.wait()
            relax_tile(r, k)
            if r < rounds - 1:
                later.append(halo_copies(r + 1, k))
                for copy in later[-1]:
                    copy.start()
            else:
                out_copies.append(remote(
                    field.at[k, pl.ds(width, cells), 1 - gy], out_ref.at[gy, k],
                    out_sems.at[0, k], out_sems.at[1, k], mate))
                out_copies[-1].start()
                out_ref[gy, k] = field[k, width:width + cells, gy]
        pending = later
    for copy in out_copies:
        copy.wait()


def fused(increments, vert_corr, kappa, sea_mask, level_count):
    levels, cells, lanes = sea_mask.shape
    tiles = levels // TILE
    width = WIDTH
    rows = cells + 2 * width
    rounds = PASSES // width
    lev = lax.axis_index("lev")
    numbers = lev * levels + jnp.arange(levels, dtype=jnp.int32)
    turned = jnp.swapaxes(sea_mask, 0, 1)
    wet = (turned * (numbers[None, :, None] < level_count[:, None, :]).astype(jnp.int32)).astype(jnp.float32)
    masked = jnp.swapaxes(increments[0], 1, 2) * wet[None]
    vmem = pl.BlockSpec(memory_space=pltpu.VMEM)
    f32 = jnp.float32
    dma = pltpu.SemaphoreType.DMA
    result = pl.pallas_call(
        kernel,
        out_shape=jax.ShapeDtypeStruct((2, tiles, cells, TILE, lanes), f32),
        in_specs=[vmem] * 4,
        out_specs=vmem,
        scratch_shapes=[
            pltpu.VMEM((2, rows, levels + TILE, lanes), f32),
            pltpu.VMEM((cells, levels, lanes), f32),
            pltpu.VMEM((2, cells, levels, lanes), f32),
            pltpu.VMEM((tiles, rows, 2, TILE, lanes), f32),
            pltpu.VMEM((rounds, 2, tiles, width, 2, TILE, lanes), f32),
            pltpu.VMEM((rows, 2, TILE, lanes), f32),
            pltpu.VMEM((rows, 2, TILE, lanes), f32),
            dma((2, 3)),
            dma((2, 3)),
            dma((2, 3)),
            dma((2, 5)),
            dma((2, rounds, 2, tiles)),
            dma((2, tiles)),
        ],
        compiler_params=pltpu.CompilerParams(
            collective_id=0, has_side_effects=True, vmem_limit_bytes=32 * 1024 * 1024
        ),
        cost_estimate=pl.CostEstimate(flops=60_000_000, bytes_accessed=4_000_000, transcendentals=0),
    )(masked, wet, vert_corr, kappa)
    return result.transpose(0, 1, 3, 2, 4).reshape(increments.shape)


def fits(mesh):
    shape = mesh.shape
    return shape["lev"] == 2 and shape["gy"] == 2 and shape["gx"] > 2


def solution(mesh):
    in_specs = (
        P(None, None, "lev", "gx", "gy"),
        P(),
        P(None, "gx", "gy"),
        P("lev", "gx", "gy"),
        P("gx", "gy"),
    )
    out_specs = P(None, None, "lev", "gx", "gy")
    return jax.shard_map(
        fused if fits(mesh) else per_device, mesh=mesh, in_specs=in_specs, out_specs=out_specs, check_vma=False
    )
```
